256 devices in a mesh: ctx: 64 (over z, y_lo, x), tp: 4 (over y_hi, core).
Axes of the slice: x: 4, y: 4 (y_hi: 2, y_lo: 2; y = y_hi * 2 + y_lo), z: 8, core: 2. Of those that a mesh axis runs over, the one named last changes fastest.
Arguments:
- queries: bfloat16 [512, 4096], P('ctx', 'tp'), may hold values from -48 to 48
- suffix_keys: bfloat16 [512, 1024], P('ctx', 'tp'), may hold values from -12 to 12
- suffix_values: bfloat16 [512, 1024], P('ctx', 'tp'), may hold values from -6 to 6
- prefix_keys: bfloat16 [262144, 1024], P('ctx', 'tp'), may hold values from -6 to 6
- prefix_values: bfloat16 [262144, 1024], P('ctx', 'tp'), may hold values from -6 to 6
- lengths: int32 [8], replicated, may hold values from 1 to 64, 384 in all
- parents: int32 [8], replicated, may hold values from 0 to 7, as said below
- out_weight: bfloat16 [4096, 4096], P('tp', 'ctx'), may hold values from -0.5 to 0.5
- residual: bfloat16 [512, 4096], P('tp', 'ctx'), may hold values from -6 to 6
Outputs:
- layer_state: bfloat16 [512, 4096], P('tp', 'ctx')
The draws below stay inside these ranges and needn't reach their ends.
Inputs may be any that keep to these rules, and one draw needn't show every extreme that they name: parents[j] <= j; parents[j] == j marks a leaf that follows the prefix directly.
All inputs are finite; a program needn't handle non-finite values.
Results may differ from the reference program's by a relative error of at most 0.006.
Values may be sent and summed in bfloat16 or wider, within the bound.
A program may use at most 320 MiB of HBM per device.

```python
import math
import jax
import jax.numpy as jnp
import numpy as np
from jax import lax

D = 4096
H = 32
KVH = 8
HD = 128
LEAVES = 8
SUF = 64
PRE_DEV = 4096
TOKENS = 512
PREFIX = 262144
LIVE = 384
N_CTX = 64


def draw_queries(key, part):
    key = jax.random.fold_in(key, 7)
    shape = (TOKENS, H * HD)
    values = jnp.clip(3.0 * jax.random.normal(key, shape, jnp.float32), -18.0, 18.0)
    return values.astype(jnp.bfloat16)


def draw_parents(key, part):
    key = jax.random.fold_in(key, 13)
    leaf_ids = jnp.arange(LEAVES, dtype=jnp.int32)
    picks = jax.random.randint(key, (LEAVES,), 0, leaf_ids + 1, dtype=jnp.int32)
    return jnp.where(leaf_ids == LEAVES - 1, LEAVES - 1, picks).astype(jnp.int32)


def levels(rng, dims, shards, smallest, top_value):
    loudness, own = 1.0, jax.random.fold_in(rng, 6)
    for dim, shards_of in shards:
        draws = jnp.exp(jax.random.uniform(jax.random.fold_in(own, dim), (shards_of,), jnp.float32, smallest / len(shards), top_value / len(shards)))
        loudness = loudness * jnp.repeat(draws, dims[dim] // shards_of).reshape([-1 if axis == dim else 1 for axis in range(len(dims))])
    return loudness


def length_profile(count, total, most, skew):
    portions = [(1 << 20) // math.isqrt(rank ** skew) + 1 for rank in range(2, count + 1)]
    surplus, counts = total - most - (count - 1), [1] * (count - 1)
    while surplus > 0:
        candidates = [i for i in range(count - 1) if counts[i] < most]
        mass, left = sum([portions[i] for i in candidates]), surplus
        for i in candidates:
            extra = min(most - counts[i], max(1, left * portions[i] // mass), surplus)
            counts[i] = counts[i] + extra
            surplus = surplus - extra
    return np.array([most] + counts)


def ragged(own_key, count, total, bound, skew):
    if count == 2:
        one = jax.random.randint(own_key, (), max(1, total - bound), min(bound, total - 1) + 1)
        return jnp.stack([one, total - one])
    tallies = jnp.asarray(length_profile(count, total, bound, skew), jnp.int32)
    twos = (count - 1) // 2
    giver, taker = tallies[1:1 + 2 * twos:2], tallies[2:2 + 2 * twos:2]
    margin = jnp.minimum(giver - 1, bound - taker)
    passed = jax.random.randint(jax.random.fold_in(own_key, 1), (twos,), 0, 1 << 20) % (margin + 1)
    tallies = tallies.at[1:1 + 2 * twos:2].set(giver - passed).at[2:2 + 2 * twos:2].set(taker + passed)
    return tallies[jax.random.permutation(jax.random.fold_in(own_key, 2), count)]


def bell_draw(rng, dims, width, most, cuts=(), kind=jnp.bfloat16):
    array = width * jax.random.normal(rng, dims, jnp.float32)
    if cuts:
        array = array * levels(rng, dims, cuts, -0.22, 0.18)
    return jnp.clip(array, -most, most).astype(kind)


def setup_inputs(seed: int = 0) -> dict:
    seeds = jax.random.split(jax.random.key(seed), 10)
    queries = draw_queries(jax.random.fold_in(seeds[9], 71), 0)
    suffix_keys = bell_draw(seeds[1], (TOKENS, KVH * HD), 2.0, 12.0, ((0, 64), (1, 4)))
    suffix_values = bell_draw(seeds[2], (TOKENS, KVH * HD), 1.0, 6.0, ((0, 64), (1, 4)))
    prefix_keys = bell_draw(seeds[3], (PREFIX, KVH * HD), 1.0, 6.0, ((0, 64), (1, 4)))
    prefix_values = bell_draw(seeds[4], (PREFIX, KVH * HD), 1.0, 6.0, ((0, 64), (1, 4)))
    lengths = ragged(seeds[5], LEAVES, LIVE, SUF, 1).astype(jnp.int32)
    parents = draw_parents(jax.random.fold_in(seeds[9], 71), 0)
    out_weight = bell_draw(seeds[7], (H * HD, D), HD ** -0.5, 0.5, ((0, 4), (1, 64)))
    residual = bell_draw(seeds[8], (TOKENS, D), 1.0, 6.0, ((0, 4), (1, 64)))
    return {"queries": queries, "suffix_keys": suffix_keys, "suffix_values": suffix_values, "prefix_keys": prefix_keys, "prefix_values": prefix_values, "lengths": lengths, "parents": parents, "out_weight": out_weight, "residual": residual}


def ancestry(parents):
    leaf_count = parents.shape[0]
    leaf_ids = jnp.arange(leaf_count, dtype=jnp.int32)
    current = leaf_ids
    ancestors = jnp.zeros((leaf_count, leaf_count), jnp.int32)
    for hop_index in range(leaf_count):
        following = lax.optimization_barrier(jnp.sum(jnp.where(current[:, None] == leaf_ids[None, :], parents[None, :], 0), axis=1)).astype(jnp.int32)
        new_links = (leaf_ids[None, :] == following[:, None]) & (following != current)[:, None]
        ancestors = jnp.maximum(ancestors, new_links.astype(jnp.int32))
        current = following
    return ancestors

def visible(row_ids, lengths, parents, token_count):
    leaf_count = lengths.shape[0]
    leaf_span = token_count // leaf_count
    leaf_ids = jnp.arange(leaf_count, dtype=jnp.int32)
    key_ids = jnp.arange(token_count, dtype=jnp.int32)
    key_leaf = key_ids // leaf_span
    key_place = key_ids % leaf_span
    row_leaf = row_ids // leaf_span
    row_place = row_ids % leaf_span
    live_keys = key_place < jnp.repeat(lengths, leaf_span)
    onehot = (row_leaf[:, None] == leaf_ids[None, :]).astype(jnp.int32)
    elders = jnp.repeat(jnp.dot(onehot, ancestry(parents)), leaf_span, axis=1) > 0
    own_leaf = (row_leaf[:, None] == key_leaf[None, :]) & (key_place[None, :] <= row_place[:, None])
    return live_keys[None, :] & (elders | own_leaf)

def reference(queries, suffix_keys, suffix_values, prefix_keys, prefix_values, lengths, parents, out_weight, residual):
    inverse_root = 1.0 / math.sqrt(HD)
    per_group = H // KVH
    grouped = queries.astype(jnp.float32).reshape(TOKENS, KVH, per_group, HD)
    key_blocks = prefix_keys.reshape(N_CTX, PRE_DEV, KVH, HD)
    value_blocks = prefix_values.reshape(N_CTX, PRE_DEV, KVH, HD)

    def absorb(carry, block_pair):
        highest, totals, weighted = carry
        key_block = block_pair[0].astype(jnp.float32)
        value_block = block_pair[1].astype(jnp.float32)
        scores = jnp.einsum('qgrd,kgd->qgrk', grouped, key_block) * inverse_root
        block_peak = lax.optimization_barrier(jnp.max(scores, axis=-1))
        weights = jnp.exp(scores - block_peak[..., None]).astype(jnp.bfloat16)
        weights = lax.optimization_barrier(weights).astype(jnp.float32)
        block_total = lax.optimization_barrier(jnp.sum(weights, axis=-1))
        block_sum = jnp.einsum('qgrk,kgd->qgrd', weights, value_block)
        raised = jnp.maximum(highest, block_peak)
        before = jnp.exp(highest - raised)
        after = jnp.exp(block_peak - raised)
        new_totals = totals * before + block_total * after
        new_weighted = weighted * before[..., None] + block_sum * after[..., None]
        return ((raised, new_totals, new_weighted), None)
    start_peak = jnp.full((TOKENS, KVH, per_group), -jnp.inf, jnp.float32)
    start_total = jnp.zeros((TOKENS, KVH, per_group), jnp.float32)
    start_sum = jnp.zeros((TOKENS, KVH, per_group, HD), jnp.float32)
    (prefix_peak, prefix_total, prefix_sum), unused = lax.scan(absorb, (start_peak, start_total, start_sum), (key_blocks, value_blocks))
    row_ids = jnp.arange(TOKENS, dtype=jnp.int32)
    allowed = visible(row_ids, lengths, parents, TOKENS)[:, None, None, :]
    leaf_keys = suffix_keys.astype(jnp.float32).reshape(TOKENS, KVH, HD)
    leaf_vals = suffix_values.astype(jnp.float32).reshape(TOKENS, KVH, HD)
    leaf_scores = jnp.einsum('qgrd,kgd->qgrk', grouped, leaf_keys) * inverse_root
    leaf_peak = lax.optimization_barrier(jnp.max(jnp.where(allowed, leaf_scores, -jnp.inf), axis=-1))
    leaf_weight = jnp.where(allowed, jnp.exp(leaf_scores - leaf_peak[..., None]), 0.0).astype(jnp.bfloat16)
    leaf_weight = lax.optimization_barrier(leaf_weight).astype(jnp.float32)
    leaf_total = lax.optimization_barrier(jnp.sum(leaf_weight, axis=-1))
    leaf_sum = jnp.einsum('qgrk,kgd->qgrd', leaf_weight, leaf_vals)
    joined_peak = jnp.maximum(prefix_peak, leaf_peak)
    prefix_scale = jnp.exp(prefix_peak - joined_peak)
    leaf_scale = jnp.exp(leaf_peak - joined_peak)
    numerator = prefix_sum * prefix_scale[..., None] + leaf_sum * leaf_scale[..., None]
    denominator = prefix_total * prefix_scale + leaf_total * leaf_scale
    attention = (numerator / denominator[..., None]).reshape(TOKENS, H * HD).astype(jnp.bfloat16)
    projected = jnp.dot(attention, out_weight, preferred_element_type=jnp.float32)
    return (residual.astype(jnp.float32) + projected).astype(jnp.bfloat16)
```

```python
import math

import jax
import jax.numpy as jnp
from jax import lax
from jax.experimental import pallas as pl
from jax.experimental.pallas import tpu as pltpu
from jax.sharding import PartitionSpec as P

HD = 128
NX, NY, NZ = 4, 2, 8
NP = NX * NY
NT = 4
LEAF_ROWS = 32
ROWS = NZ * LEAF_ROWS
TAIL = 16
KEYS = 4096
TILE = 1024
SCALE = math.log2(math.e) / math.sqrt(HD)
LOW = -1e30
F32, BF16 = jnp.float32, jnp.bfloat16
MESH = pl.DeviceIdType.MESH


def split3(x):
    hi = x.astype(BF16).astype(F32)
    rest = x - hi
    mid = rest.astype(BF16).astype(F32)
    low = (rest - mid).astype(BF16).astype(F32)
    return hi, mid, low


def pack_tail(lam):
    zeros = jnp.zeros((TAIL - 6, 128), F32)
    return jnp.concatenate([*split3(lam), zeros], axis=0).astype(BF16)


def read_tail(tail):
    tail = tail.astype(F32)
    return tail[0:2] + tail[2:4] + tail[4:6]


def kernel(
    lengths, parents, q_in, sk_in, sv_in, pk_hbm, pv_hbm, w_in, res_in, out_ref,
    keys, values, sk, sv, anc, w2, q, sums, recv_a, part_b, recv_b, att, proj, recv_p,
    load_sem, qz_s, qz_r, qp_s, qp_r, a_s, a_r, b_s, b_r, gz_s, gz_r, gp_s, gp_r, t_s, t_r,
):
    c, t = lax.axis_index("ctx"), lax.axis_index("tp")
    z, p = c // NP, c % NP
    y, x = p // NX, p % NX

    def plane(j, sign):
        xx = (x + NX + sign * (j % NX)) % NX
        yy = (y + NY + sign * (j // NX)) % NY
        return yy * NX + xx

    def at_z(k, sign):
        return (z + NZ + sign * k) % NZ

    def remote(src, dst, send, recv, ctx, tp):
        return pltpu.make_async_remote_copy(
            src_ref=src, dst_ref=dst, send_sem=send, recv_sem=recv,
            device_id=(ctx, tp), device_id_type=MESH,
        )

    loads = []
    for g in range(2):
        cols = pl.ds(g * HD, HD)
        loads.append(pltpu.make_async_copy(pk_hbm.at[:, cols], keys.at[g], load_sem.at[2 * g]))
        loads.append(pltpu.make_async_copy(pv_hbm.at[:, cols], values.at[g], load_sem.at[2 * g + 1]))
    for load in loads:
        load.start()

    barrier = pltpu.get_barrier_semaphore()
    for k in range(1, NZ):
        pl.semaphore_signal(barrier, inc=1, device_id=(at_z(k, 1) * NP + p, t), device_id_type=MESH)
    for j in range(1, NP):
        pl.semaphore_signal(barrier, inc=1, device_id=(z * NP + plane(j, 1), t), device_id_type=MESH)
    for k in range(1, NT):
        pl.semaphore_signal(barrier, inc=1, device_id=(c, (t + k) % NT), device_id_type=MESH)

    own = q_in[...].astype(F32)
    for g in range(2):
        heads = [own[:, (4 * g + h) * HD : (4 * g + h + 1) * HD] for h in range(4)]
        q[g, p, z] = jnp.concatenate(heads, axis=0).astype(BF16)
    pl.semaphore_wait(barrier, NZ - 1 + NP - 1 + NT - 1)

    def q_z(g, k):
        block = q.at[g, p, z]
        return remote(block, block, qz_s.at[g, k], qz_r.at[g, k], at_z(k, 1) * NP + p, t)

    def q_p(g, j):
        block = q.at[g, p]
        return remote(block, block, qp_s.at[g, j], qp_r.at[g, j], z * NP + plane(j, 1), t)

    for g in range(2):
        for k in range(1, NZ):
            q_z(g, k).start()

    leaf_length = lengths[z]
    pad = jnp.zeros((HD - 8, HD), F32)
    own_keys, own_values = sk_in[...].astype(F32), sv_in[...].astype(F32)
    for g in range(2):
        cols = slice(g * HD, (g + 1) * HD)
        sk[g] = jnp.concatenate([own_keys[:, cols], pad], axis=0).astype(BF16)
        sv[g] = jnp.concatenate([own_values[:, cols], pad], axis=0).astype(BF16)
    for leaf in range(NZ):
        current = jnp.int32(leaf)
        linked = jnp.int32(0)
        for _ in range(NZ):
            following = parents[current]
            hit = jnp.where(following != current, jnp.int32(1), jnp.int32(0))
            linked = jnp.maximum(linked, jnp.where(following == z, hit, jnp.int32(0)))
            current = following
        anc[leaf * LEAF_ROWS : (leaf + 1) * LEAF_ROWS, :] = jnp.full((LEAF_ROWS, HD), linked, jnp.int32)
    zeros = jnp.zeros((4 * HD, 64), BF16)
    for g in range(2):
        part = w_in[g * 4 * HD : (g + 1) * 4 * HD, :]
        w2[g, 0 : 4 * HD, :] = jnp.concatenate([part, zeros], axis=1)
        w2[g, 4 * HD : 8 * HD, :] = jnp.concatenate([zeros, part], axis=1)

    for g in range(2):
        for k in range(1, NZ):
            q_z(g, k).wait_recv()
        for j in range(1, NP):
            q_p(g, j).start()
    for load in loads:
        load.wait()

    row = lax.broadcasted_iota(jnp.int32, (ROWS, HD), 0)
    lane = lax.broadcasted_iota(jnp.int32, (ROWS, HD), 1)
    place = p * 8 + lane
    live = (lane < 8) & (place < leaf_length)
    same_leaf = (row // LEAF_ROWS) == z
    eye = lax.broadcasted_iota(jnp.int32, (HD, HD), 0) == lax.broadcasted_iota(jnp.int32, (HD, HD), 1)
    ones = jnp.ones((TILE, HD), BF16)

    def send_a(g, j):
        return remote(
            sums.at[g, j], recv_a.at[g, j], a_s.at[g, j], a_r.at[g, j], z * NP + plane(j, -1), t
        )

    def attend(g, first):
        blocks, masks = [], []
        for j in (first, first + 1):
            source = plane(j, -1)
            blocks.append(q[g, source].reshape(ROWS, HD))
            own_row = same_leaf & (place <= source * 8 + row % 8)
            masks.append(jnp.where(live & (own_row | (anc[...] > 0)), 1.0, 0.0))
        scaled = jnp.concatenate(blocks, axis=0).astype(F32) * SCALE
        hi = scaled.astype(BF16)
        low = (scaled - hi.astype(F32)).astype(BF16)
        query = jnp.concatenate([hi, low], axis=1)
        allowed = jnp.concatenate(masks, axis=0) > 0.5

        def scores(block):
            return lax.dot_general(
                query, jnp.concatenate([block, block], axis=1),
                (((1,), (1,)), ((), ())), preferred_element_type=F32,
            )

        leaf_scores = jnp.where(allowed, scores(sk[g]), LOW)
        following = scores(keys[g, 0:TILE, :])
        peak = jnp.max(leaf_scores, axis=1, keepdims=True)
        weight = jnp.where(allowed, jnp.exp2(leaf_scores - peak), 0.0).astype(BF16)
        total = jnp.dot(
            weight, jnp.concatenate([sv[g], ones[:HD]], axis=1), preferred_element_type=F32
        )
        for tile in range(KEYS // TILE):
            now = following
            raised = jnp.maximum(peak, jnp.max(now, axis=1, keepdims=True))
            if tile + 1 < KEYS // TILE:
                following = scores(keys[g, (tile + 1) * TILE : (tile + 2) * TILE, :])
            weight = jnp.exp2(now - raised).astype(BF16)
            table = jnp.concatenate([values[g, tile * TILE : (tile + 1) * TILE, :], ones], axis=1)
            total = total * jnp.exp2(peak - raised) + jnp.dot(weight, table, preferred_element_type=F32)
            peak = raised
        mean = (total[:, :HD] / total[:, HD:]).astype(BF16)
        lam = (peak + jnp.log2(total[:, HD:])).reshape(2, 2, HD, HD)
        lam = jnp.sum(jnp.where(eye[None, None], lam, 0.0), axis=2)
        for i in range(2):
            sums[g, first + i, 0:ROWS, :] = mean[i * ROWS : (i + 1) * ROWS]
            sums[g, first + i, ROWS : ROWS + TAIL, :] = pack_tail(lam[i])

    def send_b(g, k):
        return remote(
            part_b.at[g, at_z(k, 1)], recv_b.at[g, k], b_s.at[g, k], b_r.at[g, k], at_z(k, 1) * NP + p, t
        )

    def merge_plane(g):
        for j in range(1, NP):
            send_a(g, j).wait_recv()
        held = [sums.at[g, 0]] + [recv_a.at[g, j] for j in range(1, NP)]
        lams = [read_tail(block[ROWS : ROWS + TAIL, :]) for block in held]
        peak = lams[0]
        for lam in lams[1:]:
            peak = jnp.maximum(peak, lam)
        weights = [jnp.exp2(lam - peak) for lam in lams]
        whole = sum(weights[1:], weights[0])
        tail = pack_tail(peak + jnp.log2(whole))
        weights = [weight / whole for weight in weights]
        for half in range(2):
            merged = None
            for block, weight in zip(held, weights):
                column = jnp.sum(jnp.where(eye, weight[half : half + 1], 0.0), axis=1, keepdims=True)
                term = column * block[half * HD : (half + 1) * HD, :].astype(F32)
                merged = term if merged is None else merged + term
            merged = merged.astype(BF16)
            for i in range(4):
                part_b[g, 4 * half + i, 0:LEAF_ROWS, :] = merged[i * LEAF_ROWS : (i + 1) * LEAF_ROWS]
                part_b[g, 4 * half + i, LEAF_ROWS : LEAF_ROWS + TAIL, :] = tail
        for k in range(1, NZ):
            send_b(g, k).start()

    def att_z(g, k):
        block = att.at[g, p, z]
        return remote(block, block, gz_s.at[g, k], gz_r.at[g, k], at_z(k, 1) * NP + p, t)

    def att_p(g, j):
        block = att.at[g, p]
        return remote(block, block, gp_s.at[g, j], gp_r.at[g, j], z * NP + plane(j, 1), t)

    def merge_z(g):
        for k in range(1, NZ):
            send_b(g, k).wait_recv()
        shape = (LEAF_ROWS, HD)
        spot = lax.broadcasted_iota(jnp.int32, shape, 1) == (
            lax.broadcasted_iota(jnp.int32, shape, 0) + LEAF_ROWS * (z % 4)
        )
        held = [part_b[g, z]] + [recv_b[g, k] for k in range(1, NZ)]
        lams = []
        for block in held:
            lam = read_tail(block[LEAF_ROWS : LEAF_ROWS + TAIL])
            line = jnp.where(z // 4 == 0, lam[0:1], lam[1:2])
            lams.append(jnp.sum(jnp.where(spot, line, 0.0), axis=1, keepdims=True))
        peak = lams[0]
        for lam in lams[1:]:
            peak = jnp.maximum(peak, lam)
        top, whole = None, None
        for block, lam in zip(held, lams):
            weight = jnp.exp2(lam - peak)
            term = weight * block[:LEAF_ROWS].astype(F32)
            top = term if top is None else top + term
            whole = weight if whole is None else whole + weight
        att[g, p, z] = (top / whole).astype(BF16)
        for k in range(1, NZ):
            att_z(g, k).start()

    def spread_plane(g):
        for k in range(1, NZ):
            att_z(g, k).wait_recv()
        for j in range(1, NP):
            att_p(g, j).start()

    def project(g):
        for j in range(1, NP):
            att_p(g, j).wait_recv()
        lines = []
        for source in range(NP):
            rows = att[g, source].astype(F32).reshape(NT, 2, 4, 8, HD)
            parts = [rows[:, side, h].reshape(NT * 8, HD) for side in range(2) for h in range(4)]
            lines.append(jnp.concatenate(parts, axis=1))
        lines = jnp.concatenate(lines, axis=0).astype(BF16)
        return jnp.dot(lines, w2[g], preferred_element_type=F32).reshape(NP, NT, 8, HD)

    def step(i, carry):
        g, first = i // 4, (i % 4) * 2

        for j in (first, first + 1):

            @pl.when(j > 0)
            def _():
                q_p(g, j).wait_recv()

        @pl.when(i == 5)
        def _():
            merge_plane(0)

        @pl.when(i == 6)
        def _():
            merge_z(0)

        @pl.when(i == 7)
        def _():
            spread_plane(0)

        attend(g, first)
        for j in (first, first + 1):

            @pl.when(j > 0)
            def _():
                send_a(g, j).start()

        return carry

    lax.fori_loop(0, 8, step, 0)
    merge_plane(1)
    merge_z(1)
    spread_plane(1)
    projected = project(0)
    projected = projected + project(1)

    def share(k):
        to = (t + k) % NT
        return remote(proj.at[to], recv_p.at[k], t_s.at[k], t_r.at[k], c, to)

    for to in range(NT):
        proj[to] = projected[:, to]
    for k in range(1, NT):
        share(k).start()
    for k in range(1, NT):
        share(k).wait_recv()
    total = proj[t]
    for k in range(1, NT):
        total = total + recv_p[k]
    total = total.reshape(NP * 8, HD)
    out_ref[0:64, :] = (res_in[0:64, :].astype(F32) + total[:, :64]).astype(BF16)
    out_ref[64:128, :] = (res_in[64:128, :].astype(F32) + total[:, 64:]).astype(BF16)

    for g in range(2):
        for k in range(1, NZ):
            q_z(g, k).wait_send()
            send_b(g, k).wait_send()
            att_z(g, k).wait_send()
        for j in range(1, NP):
            q_p(g, j).wait_send()
            send_a(g, j).wait_send()
            att_p(g, j).wait_send()
    for k in range(1, NT):
        share(k).wait_send()


def shards(queries, suffix_keys, suffix_values, prefix_keys, prefix_values, lengths, parents, out_weight, residual):
    vmem, smem, hbm = (
        pl.BlockSpec(memory_space=pltpu.VMEM),
        pl.BlockSpec(memory_space=pltpu.SMEM),
        pl.BlockSpec(memory_space=pl.ANY),
    )
    dma = pltpu.SemaphoreType.DMA
    return pl.pallas_call(
        kernel,
        out_shape=jax.ShapeDtypeStruct(residual.shape, BF16),
        in_specs=[smem, smem, vmem, vmem, vmem, hbm, hbm, vmem, vmem],
        out_specs=vmem,
        scratch_shapes=[
            pltpu.VMEM((2, KEYS, HD), BF16),
            pltpu.VMEM((2, KEYS, HD), BF16),
            pltpu.VMEM((2, HD, HD), BF16),
            pltpu.VMEM((2, HD, HD), BF16),
            pltpu.VMEM((ROWS, HD), jnp.int32),
            pltpu.VMEM((2, 8 * HD, HD), BF16),
            pltpu.VMEM((2, NP, NZ, LEAF_ROWS, HD), BF16),
            pltpu.VMEM((2, NP, ROWS + TAIL, HD), BF16),
            pltpu.VMEM((2, NP, ROWS + TAIL, HD), BF16),
            pltpu.VMEM((2, NZ, LEAF_ROWS + TAIL, HD), BF16),
            pltpu.VMEM((2, NZ, LEAF_ROWS + TAIL, HD), BF16),
            pltpu.VMEM((2, NP, NZ, LEAF_ROWS, HD), BF16),
            pltpu.VMEM((NT, NP, 8, HD), F32),
            pltpu.VMEM((NT, NP, 8, HD), F32),
            dma((4,)),
            dma((2, NZ)), dma((2, NZ)),
            dma((2, NP)), dma((2, NP)),
            dma((2, NP)), dma((2, NP)),
            dma((2, NZ)), dma((2, NZ)),
            dma((2, NZ)), dma((2, NZ)),
            dma((2, NP)), dma((2, NP)),
            dma((NT,)), dma((NT,)),
        ],
        compiler_params=pltpu.CompilerParams(
            collective_id=0, has_side_effects=True, vmem_limit_bytes=48 << 20
        ),
        cost_estimate=pl.CostEstimate(
            flops=18 << 30, bytes_accessed=5 << 20, transcendentals=17 << 20
        ),
        name="cascade",
    )(lengths, parents, queries, suffix_keys, suffix_values, prefix_keys, prefix_values, out_weight, residual)


def solution(mesh):
    placed = (
        P("ctx", "tp"), P("ctx", "tp"), P("ctx", "tp"), P("ctx", "tp"), P("ctx", "tp"),
        P(), P(), P("tp", "ctx"), P("tp", "ctx"),
    )
    return jax.shard_map(shards, mesh=mesh, in_specs=placed, out_specs=P("tp", "ctx"), check_vma=False)
```

```python
import math

import jax
import jax.numpy as jnp
from jax import lax
from jax.experimental import pallas as pl
from jax.experimental.pallas import tpu as pltpu
from jax.sharding import PartitionSpec as P

HD = 128
NX, NY, NZ = 4, 2, 8
NP = NX * NY
NT = 4
LEAF_ROWS = 32
ROWS = NZ * LEAF_ROWS
TAIL = 16
KEYS = 4096
TILE = 1024
SCALE = math.log2(math.e) / math.sqrt(HD)
LOW = -1e30
F32, BF16 = jnp.float32, jnp.bfloat16
MESH = pl.DeviceIdType.MESH


def split3(x):
    hi = x.astype(BF16).astype(F32)
    rest = x - hi
    mid = rest.astype(BF16).astype(F32)
    low = (rest - mid).astype(BF16).astype(F32)
    return hi, mid, low


def pack_tail(lam):
    zeros = jnp.zeros((TAIL - 6, 128), F32)
    return jnp.concatenate([*split3(lam), zeros], axis=0).astype(BF16)


def read_tail(tail):
    tail = tail.astype(F32)
    return tail[0:2] + tail[2:4] + tail[4:6]


def kernel(
    lengths_in, parents_in, q_hbm, sk_hbm, sv_hbm, pk_hbm, pv_hbm, w_hbm, res_hbm, out_ref,
    lengths, parents, q_in, sk_in, sv_in, res_in, keys, values, weights, sk, sv, anc, q, sums, recv_y, recv_x, part_b, recv_b, att,
    shares_out, shares_in,
    load_sem, qz_s, qz_r, qx_s, qx_r, qh_s, qh_r, qy_s, qy_r, w_s, w_r, ay_s, ay_r, ax_s, ax_r, b_s, b_r, c_s, c_r, d_s, d_r,
):
    far_first = (4, 3, 5, 2, 6, 1, 7)
    c, t = lax.axis_index("ctx"), lax.axis_index("tp")
    z, p = c // NP, c % NP
    y, x = p // NX, p % NX

    def plane(j, sign):
        xx = (x + NX + sign * (j % NX)) % NX
        yy = (y + NY + sign * (j // NX)) % NY
        return yy * NX + xx

    def at_z(k, sign):
        return (z + NZ + sign * k) % NZ

    def remote(src, dst, send, recv, ctx, tp):
        return pltpu.make_async_remote_copy(
            src_ref=src, dst_ref=dst, send_sem=send, recv_sem=recv,
            device_id=(ctx, tp), device_id_type=MESH,
        )

    early = pltpu.make_async_copy(q_hbm, q_in, load_sem.at[4])
    early.start()
    loads = []
    for k, (src, dst) in enumerate(
        ((lengths_in, lengths), (parents_in, parents), (sk_hbm, sk_in), (sv_hbm, sv_in), (w_hbm, weights.at[z]), (res_hbm, res_in))
    ):
        loads.append(pltpu.make_async_copy(src, dst, load_sem.at[5 + k]))
    for g in range(2):
        cols = pl.ds(g * HD, HD)
        loads.append(pltpu.make_async_copy(pk_hbm.at[:, cols], keys.at[g], load_sem.at[2 * g]))
        loads.append(pltpu.make_async_copy(pv_hbm.at[:, cols], values.at[g], load_sem.at[2 * g + 1]))
    for load in loads:
        load.start()

    barrier = pltpu.get_barrier_semaphore()
    for k in (*far_first, 0):
        for i in range(NT):
            if k or i:
                there = (at_z(k, 1) * NP + p, (t + i) % NT)
                pl.semaphore_signal(barrier, inc=1, device_id=there, device_id_type=MESH)
    for j in range(1, NP):
        pl.semaphore_signal(barrier, inc=1, device_id=(z * NP + plane(j, 1), t), device_id_type=MESH)

    early.wait()
    own = q_in[...].astype(F32)
    for g in range(2):
        heads = [own[:, (4 * g + h) * HD : (4 * g + h + 1) * HD] for h in range(4)]
        q[g, p, z] = jnp.concatenate(heads, axis=0).astype(BF16)
    pl.semaphore_wait(barrier, NZ * NT - 1 + NP - 1)

    def q_z(g, k):
        block = q.at[g, p, z]
        return remote(block, block, qz_s.at[g, k], qz_r.at[g, k], at_z(k, 1) * NP + p, t)

    across = z * NP + (1 - y) * NX + x

    def q_x(g, j):
        block = q.at[g, plane(j - j % NX, -1)]
        return remote(block, block, qx_s.at[g, j], qx_r.at[g, j], z * NP + plane(j % NX, 1), t)

    def q_half(g, side):
        j = 1 + 2 * side
        block = q.at[g, plane(j, -1), pl.ds(side * 4, 4)]
        return remote(block, block, qh_s.at[g, side], qh_r.at[g, side], z * NP + plane(j, 1), t)

    def q_y(g, j):
        block = q.at[g, plane(j, -1)]
        return remote(block, block, qy_s.at[g, j], qy_r.at[g, j], across, t)

    def round_1(g):
        for k in far_first:
            q_z(g, k).wait_recv()
        q_x(g, 1).start()
        q_x(g, 3).start()
        q_y(g, 0).start()

    def round_2(g):
        for j in (1, 3):
            q_x(g, j).wait_recv()
        q_half(g, 0).start()
        q_half(g, 1).start()
        q_y(g, 0).wait_recv()
        q_x(g, 5).start()
        q_x(g, 7).start()

    def round_3(g):
        q_half(g, 0).wait_recv()
        q_half(g, 1).wait_recv()
        q_y(g, 2).start()

    def pass_w(hop, sign):
        block = weights.at[at_z(hop - 1, -sign)]
        side = (1 - sign) // 2
        return remote(block, block, w_s.at[side, hop], w_r.at[side, hop], at_z(1, sign) * NP + p, t)

    for k in far_first:
        q_z(0, k).start()

    for load in loads:
        load.wait()
    leaf_length = lengths[z]
    pad = jnp.zeros((HD - 8, HD), F32)
    own_keys, own_values = sk_in[...].astype(F32), sv_in[...].astype(F32)
    for g in range(2):
        cols = slice(g * HD, (g + 1) * HD)
        sk[g] = jnp.concatenate([own_keys[:, cols], pad], axis=0).astype(BF16)
        sv[g] = jnp.concatenate([own_values[:, cols], pad], axis=0).astype(BF16)
    for leaf in range(NZ):
        current = jnp.int32(leaf)
        linked = jnp.int32(0)
        for _ in range(NZ):
            following = parents[current]
            hit = jnp.where(following != current, jnp.int32(1), jnp.int32(0))
            linked = jnp.maximum(linked, jnp.where(following == z, hit, jnp.int32(0)))
            current = following
        anc[leaf * LEAF_ROWS : (leaf + 1) * LEAF_ROWS, :] = jnp.full((LEAF_ROWS, HD), linked, jnp.int32)
    round_1(0)
    for k in far_first:
        q_z(1, k).start()
    pass_w(1, 1).start()
    pass_w(1, -1).start()

    row = lax.broadcasted_iota(jnp.int32, (ROWS, HD), 0)
    lane = lax.broadcasted_iota(jnp.int32, (ROWS, HD), 1)
    place = p * 8 + lane
    live = (lane < 8) & (place < leaf_length)
    same_leaf = (row // LEAF_ROWS) == z
    eye = lax.broadcasted_iota(jnp.int32, (HD, HD), 0) == lax.broadcasted_iota(jnp.int32, (HD, HD), 1)
    ones = jnp.ones((TILE, HD), BF16)

    def send_y(g, j):
        return remote(sums.at[g, NX + j], recv_y.at[g, j], ay_s.at[g, j], ay_r.at[g, j], across, t)

    def send_x(g, j):
        return remote(sums.at[g, j], recv_x.at[g, j], ax_s.at[g, j], ax_r.at[g, j], z * NP + plane(j, -1), t)

    def attend(g, pair):
        blocks, masks = [], []
        for j in pair:
            source = plane(j, -1)
            blocks.append(q[g, source].reshape(ROWS, HD))
            own_row = same_leaf & (place <= source * 8 + row % 8)
            masks.append(jnp.where(live & (own_row | (anc[...] > 0)), 1.0, 0.0))
        scaled = jnp.concatenate(blocks, axis=0).astype(F32) * SCALE
        hi = scaled.astype(BF16)
        low = (scaled - hi.astype(F32)).astype(BF16)
        query = jnp.concatenate([hi, low], axis=1)
        allowed = jnp.concatenate(masks, axis=0) > 0.5

        def scores(block):
            return lax.dot_general(
                query, jnp.concatenate([block, block], axis=1),
                (((1,), (1,)), ((), ())), preferred_element_type=F32,
            )

        leaf_scores = jnp.where(allowed, scores(sk[g]), LOW)
        following = scores(keys[g, 0:TILE, :])
        peak = jnp.max(leaf_scores, axis=1, keepdims=True)
        weight = jnp.where(allowed, jnp.exp2(leaf_scores - peak), 0.0).astype(BF16)
        total = jnp.dot(
            weight, jnp.concatenate([sv[g], ones[:HD]], axis=1), preferred_element_type=F32
        )
        for tile in range(KEYS // TILE):
            now = following
            raised = jnp.maximum(peak, jnp.max(now, axis=1, keepdims=True))
            if tile + 1 < KEYS // TILE:
                following = scores(keys[g, (tile + 1) * TILE : (tile + 2) * TILE, :])
            weight = jnp.exp2(now - raised).astype(BF16)
            table = jnp.concatenate([values[g, tile * TILE : (tile + 1) * TILE, :], ones], axis=1)
            total = total * jnp.exp2(peak - raised) + jnp.dot(weight, table, preferred_element_type=F32)
            peak = raised
        mean = (total[:, :HD] / total[:, HD:]).astype(BF16)
        lam = (peak + jnp.log2(total[:, HD:])).reshape(2, 2, HD, HD)
        lam = jnp.sum(jnp.where(eye[None, None], lam, 0.0), axis=2)
        for i, j in enumerate(pair):
            sums[g, j, 0:ROWS, :] = mean[i * ROWS : (i + 1) * ROWS]
            sums[g, j, ROWS : ROWS + TAIL, :] = pack_tail(lam[i])

    def send_b(g, k):
        return remote(
            part_b.at[g, at_z(k, 1)], recv_b.at[g, k], b_s.at[g, k], b_r.at[g, k], at_z(k, 1) * NP + p, t
        )

    def merge_pair(g, j):
        send_y(g, j).wait_recv()
        ours, theirs = sums.at[g, j], recv_y.at[g, j]
        lam_a, lam_b = read_tail(ours[ROWS : ROWS + TAIL, :]), read_tail(theirs[ROWS : ROWS + TAIL, :])
        peak = jnp.maximum(lam_a, lam_b)
        whole = peak + jnp.log2(jnp.exp2(lam_a - peak) + jnp.exp2(lam_b - peak))
        weight = jnp.exp2(lam_a - whole)
        for half in range(2):
            span = slice(half * HD, (half + 1) * HD)
            column = jnp.sum(jnp.where(eye, weight[half : half + 1], 0.0), axis=1, keepdims=True)
            a, b = ours[span, :].astype(F32), theirs[span, :].astype(F32)
            ours[span, :] = (b + column * (a - b)).astype(BF16)
        ours[ROWS : ROWS + TAIL, :] = pack_tail(whole)
        if j:
            send_x(g, j).start()

    def merge_plane(g):
        for j in range(1, NX):
            send_x(g, j).wait_recv()
        held = [sums.at[g, 0]] + [recv_x.at[g, j] for j in range(1, NX)]
        lams = [read_tail(block[ROWS : ROWS + TAIL, :]) for block in held]
        peak = lams[0]
        for lam in lams[1:]:
            peak = jnp.maximum(peak, lam)
        weights = [jnp.exp2(lam - peak) for lam in lams]
        whole = sum(weights[1:], weights[0])
        tail = pack_tail(peak + jnp.log2(whole))
        weights = [weight / whole for weight in weights]
        for half in range(2):
            merged = None
            for block, weight in zip(held, weights):
                column = jnp.sum(jnp.where(eye, weight[half : half + 1], 0.0), axis=1, keepdims=True)
                term = column * block[half * HD : (half + 1) * HD, :].astype(F32)
                merged = term if merged is None else merged + term
            merged = merged.astype(BF16)
            for i in range(4):
                part_b[g, 4 * half + i, 0:LEAF_ROWS, :] = merged[i * LEAF_ROWS : (i + 1) * LEAF_ROWS]
                part_b[g, 4 * half + i, LEAF_ROWS : LEAF_ROWS + TAIL, :] = tail
        for k in far_first:
            send_b(g, k).start()

    def att_p(g, j):
        block = att.at[g, p]
        return remote(block, block, c_s.at[g, j], c_r.at[g, j], z * NP + plane(j, 1), t)

    def merge_z(g):
        for k in range(1, NZ):
            send_b(g, k).wait_recv()
        shape = (LEAF_ROWS, HD)
        spot = lax.broadcasted_iota(jnp.int32, shape, 1) == (
            lax.broadcasted_iota(jnp.int32, shape, 0) + LEAF_ROWS * (z % 4)
        )
        held = [part_b[g, z]] + [recv_b[g, k] for k in range(1, NZ)]
        lams = []
        for block in held:
            lam = read_tail(block[LEAF_ROWS : LEAF_ROWS + TAIL])
            line = jnp.where(z // 4 == 0, lam[0:1], lam[1:2])
            lams.append(jnp.sum(jnp.where(spot, line, 0.0), axis=1, keepdims=True))
        peak = lams[0]
        for lam in lams[1:]:
            peak = jnp.maximum(peak, lam)
        top, whole = None, None
        for block, lam in zip(held, lams):
            weight = jnp.exp2(lam - peak)
            term = weight * block[:LEAF_ROWS].astype(F32)
            top = term if top is None else top + term
            whole = weight if whole is None else whole + weight
        att[g, p] = (top / whole).astype(BF16)
        for j in (6, 5, 7, 2, 4, 1, 3):
            att_p(g, j).start()

    def project(g):
        for j in range(1, NP):
            att_p(g, j).wait_recv()
        rows = [att[g, source].astype(F32) for source in range(NP)]
        heads = []
        for h in range(4):
            heads.append(jnp.concatenate([block[8 * h : 8 * h + 8] for block in rows], axis=0))
        tokens = jnp.concatenate(heads, axis=1).astype(BF16)
        table = weights[:, :, g * 4 * HD : (g + 1) * 4 * HD].reshape(NZ * 64, 4 * HD)
        return lax.dot_general(table, tokens, (((1,), (1,)), ((), ())), preferred_element_type=F32)

    def step(i, carry):
        g, k = i // 4, i % 4

        def of_step(table):
            values = []
            for a, b, c, d in table:
                second, third = c - 2 * b + a, d - 3 * c + 3 * b - a
                value = a + (b - a) * k + second * (k * (k - 1) // 2) + third * (k * (k - 1) * (k - 2) // 6)
                values.append(value)
            return values[0] * (1 - g) + values[1] * g

        pair = (of_step(((0, 3, 5, 2), (5, 1, 2, 0))), of_step(((1, 4, 7, 6), (7, 6, 3, 4))))

        @pl.when(i == 0)
        def _():
            round_2(0)
            round_1(1)

        @pl.when(i == 1)
        def _():
            round_3(0)

        @pl.when(i == 2)
        def _():
            round_2(1)
            q_x(0, 5).wait_recv()
            q_x(0, 7).wait_recv()

        @pl.when(i == 3)
        def _():
            q_y(0, 2).wait_recv()
            round_3(1)

        @pl.when(i == 4)
        def _():
            q_x(1, 5).wait_recv()
            q_x(1, 7).wait_recv()

        @pl.when(i == 5)
        def _():
            q_y(1, 2).wait_recv()

        for hop in (2, 3, 4):

            @pl.when(i == 2 * hop - 2)
            def _():
                pass_w(hop - 1, 1).wait_recv()
                pass_w(hop, 1).start()
                pass_w(hop - 1, -1).wait_recv()
                if hop < 4:
                    pass_w(hop, -1).start()

        @pl.when(i == 6)
        def _():
            for j in (2, 1, 3, 0):
                merge_pair(0, j)

        @pl.when(i == 7)
        def _():
            merge_pair(1, 1)
            merge_pair(1, 3)
            merge_pair(1, 2)

        attend(g, pair)
        for j in pair:

            @pl.when(j >= NX)
            def _():
                send_y(g, j - NX).start()

        return carry

    lax.fori_loop(0, 8, step, 0)
    merge_plane(0)
    merge_pair(1, 0)
    merge_plane(1)
    merge_z(0)
    merge_z(1)
    pass_w(4, 1).wait_recv()
    projected = project(0)
    projected = projected + project(1)
    for k in range(NZ):
        block = projected[64 * k : 64 * k + 64]
        shares_out[k] = jnp.concatenate([block[:32], block[32:]], axis=1).astype(BF16)

    home = z // 2
    slot = (z % 2) * NT + t

    def share(k):
        to = at_z(k, 1)
        return remote(shares_out.at[to], shares_in.at[slot], d_s.at[k], d_r.at[slot], to * NP + p, home)

    stays = home == t
    for k in far_first:
        share(k).start()

    @pl.when(jnp.logical_not(stays))
    def _():
        share(0).start()

    @pl.when(stays)
    def _():
        shares_in[slot] = shares_out[z]

    for side in range(2):
        for i in range(NT):

            @pl.when(jnp.logical_not((2 * t + side == z) & (t == i)))
            def _():
                here = shares_in.at[side * NT + i]
                remote(here, here, d_s.at[0], d_r.at[side * NT + i], (2 * t + side) * NP + p, i).wait_recv()

    sides = []
    for side in range(2):
        parts = [shares_in[side * NT + i].astype(F32) for i in range(NT)]
        sides.append((parts[0] + parts[1]) + (parts[2] + parts[3]))
    top = jnp.concatenate([sides[0][:, :64], sides[1][:, :64]], axis=1)
    bottom = jnp.concatenate([sides[0][:, 64:], sides[1][:, 64:]], axis=1)
    out_ref[0:32, :] = (res_in[0:32, :].astype(F32) + top).astype(BF16)
    out_ref[32:64, :] = (res_in[32:64, :].astype(F32) + bottom).astype(BF16)

    for g in range(2):
        for k in range(1, NZ):
            q_z(g, k).wait_send()
            send_b(g, k).wait_send()
        for j in range(1, NP):
            att_p(g, j).wait_send()
        for j in (1, 3, 5, 7):
            q_x(g, j).wait_send()
        for side in range(2):
            q_half(g, side).wait_send()
            q_y(g, 2 * side).wait_send()
        for j in range(NX):
            send_y(g, j).wait_send()
        for j in range(1, NX):
            send_x(g, j).wait_send()
    for hop in range(1, 5):
        pass_w(hop, 1).wait_send()
        if hop < 4:
            pass_w(hop, -1).wait_send()
    for k in range(1, NZ):
        share(k).wait_send()

    @pl.when(jnp.logical_not(stays))
    def _():
        share(0).wait_send()


def shards(queries, suffix_keys, suffix_values, prefix_keys, prefix_values, lengths, parents, out_weight, residual):
    hbm = pl.BlockSpec(memory_space=pltpu.HBM)
    dma = pltpu.SemaphoreType.DMA
    flipped = pl.pallas_call(
        kernel,
        out_shape=jax.ShapeDtypeStruct(residual.shape[::-1], BF16),
        in_specs=[hbm] * 9,
        out_specs=pl.BlockSpec(memory_space=pltpu.VMEM),
        scratch_shapes=[
            pltpu.SMEM((8,), jnp.int32),
            pltpu.SMEM((8,), jnp.int32),
            pltpu.VMEM((8, 8 * HD), BF16),
            pltpu.VMEM((8, 2 * HD), BF16),
            pltpu.VMEM((8, 2 * HD), BF16),
            pltpu.VMEM((64, HD), BF16),
            pltpu.VMEM((2, KEYS, HD), BF16),
            pltpu.VMEM((2, KEYS, HD), BF16),
            pltpu.VMEM((NZ, 64, 8 * HD), BF16),
            pltpu.VMEM((2, HD, HD), BF16),
            pltpu.VMEM((2, HD, HD), BF16),
            pltpu.VMEM((ROWS, HD), jnp.int32),
            pltpu.VMEM((2, NP, NZ, LEAF_ROWS, HD), BF16),
            pltpu.VMEM((2, NP, ROWS + TAIL, HD), BF16),
            pltpu.VMEM((2, NX, ROWS + TAIL, HD), BF16),
            pltpu.VMEM((2, NX, ROWS + TAIL, HD), BF16),
            pltpu.VMEM((2, NZ, LEAF_ROWS + TAIL, HD), BF16),
            pltpu.VMEM((2, NZ, LEAF_ROWS + TAIL, HD), BF16),
            pltpu.VMEM((2, NP, LEAF_ROWS, HD), BF16),
            pltpu.VMEM((NZ, 32, HD), BF16),
            pltpu.VMEM((2 * NT, 32, HD), BF16),
            dma((11,)),
            dma((2, NZ)), dma((2, NZ)),
            dma((2, NP)), dma((2, NP)),
            dma((2, 2)), dma((2, 2)),
            dma((2, NX)), dma((2, NX)),
            dma((2, 5)), dma((2, 5)),
            dma((2, NX)), dma((2, NX)),
            dma((2, NX)), dma((2, NX)),
            dma((2, NZ)), dma((2, NZ)),
            dma((2, NP)), dma((2, NP)),
            dma((NZ,)), dma((2 * NT,)),
        ],
        compiler_params=pltpu.CompilerParams(
            collective_id=0, has_side_effects=True, vmem_limit_bytes=(64 << 20) - (64 << 10)
        ),
        cost_estimate=pl.CostEstimate(
            flops=18 << 30, bytes_accessed=5 << 20, transcendentals=17 << 20
        ),
        name="cascade",
    )(lengths, parents, queries, suffix_keys, suffix_values, prefix_keys, prefix_values, out_weight.T, residual.T)
    return flipped.T


def solution(mesh):
    placed = (
        P("ctx", "tp"), P("ctx", "tp"), P("ctx", "tp"), P("ctx", "tp"), P("ctx", "tp"),
        P(), P(), P("tp", "ctx"), P("tp", "ctx"),
    )
    return jax.shard_map(shards, mesh=mesh, in_specs=placed, out_specs=P("tp", "ctx"), check_vma=False)
```

```python
import math

import jax
import jax.numpy as jnp
from jax import lax
from jax.experimental import pallas as pl
from jax.experimental.pallas import tpu as pltpu
from jax.sharding import PartitionSpec as P

HD = 128
NX, NY, NZ = 4, 2, 8
NP = NX * NY
NT = 4
LEAF_ROWS = 32
ROWS = NZ * LEAF_ROWS
TAIL = 16
KEYS = 4096
TILE = 1024
SCALE = math.log2(math.e) / math.sqrt(HD)
LOW = -1e30
F32, BF16 = jnp.float32, jnp.bfloat16
MESH = pl.DeviceIdType.MESH


def split3(x):
    hi = x.astype(BF16).astype(F32)
    rest = x - hi
    mid = rest.astype(BF16).astype(F32)
    low = (rest - mid).astype(BF16).astype(F32)
    return hi, mid, low


def pack_tail(lam):
    zeros = jnp.zeros((TAIL - 6, 128), F32)
    return jnp.concatenate([*split3(lam), zeros], axis=0).astype(BF16)


def read_tail(tail):
    tail = tail.astype(F32)
    return tail[0:2] + tail[2:4] + tail[4:6]


def kernel(
    lengths_in, parents_in, q_hbm, sk_hbm, sv_hbm, pk_hbm, pv_hbm, w_hbm, res_hbm, out_ref,
    lengths, parents, q_in, sk_in, sv_in, res_in, keys, values, weights, sk, sv, anc, q, sums, recv_y, recv_x, part_b, recv_b, att,
    shares_out, shares_in,
    load_sem, qz_s, qz_r, qx_s, qx_r, qh_s, qh_r, qy_s, qy_r, w_s, w_r, ay_s, ay_r, ax_s, ax_r, b_s, b_r, c_s, c_r, d_s, d_r,
):
    far_first = (4, 3, 5, 2, 6, 1, 7)
    c, t = lax.axis_index("ctx"), lax.axis_index("tp")
    z, p = c // NP, c % NP
    y, x = p // NX, p % NX

    def plane(j, sign):
        xx = (x + NX + sign * (j % NX)) % NX
        yy = (y + NY + sign * (j // NX)) % NY
        return yy * NX + xx

    def at_z(k, sign):
        return (z + NZ + sign * k) % NZ

    def remote(src, dst, send, recv, ctx, tp):
        return pltpu.make_async_remote_copy(
            src_ref=src, dst_ref=dst, send_sem=send, recv_sem=recv,
            device_id=(ctx, tp), device_id_type=MESH,
        )

    early = pltpu.make_async_copy(q_hbm, q_in, load_sem.at[4])
    early.start()
    barrier = pltpu.get_barrier_semaphore()
    for k in far_first:
        pl.semaphore_signal(barrier, inc=1, device_id=(at_z(k, 1) * NP + p, t), device_id_type=MESH)
    for j in range(1, NP):
        pl.semaphore_signal(barrier, inc=1, device_id=(z * NP + plane(j, 1), t), device_id_type=MESH)
    for side in range(2):
        for i in range(1, NT):
            there = ((2 * t + side) * NP + p, (t + i) % NT)
            pl.semaphore_signal(barrier, inc=1, device_id=there, device_id_type=MESH)

    loads = []
    for k, (src, dst) in enumerate(
        ((lengths_in, lengths), (parents_in, parents), (sk_hbm, sk_in), (sv_hbm, sv_in), (w_hbm, weights.at[z]), (res_hbm, res_in))
    ):
        loads.append(pltpu.make_async_copy(src, dst, load_sem.at[5 + k]))
    for g in range(2):
        cols = pl.ds(g * HD, HD)
        loads.append(pltpu.make_async_copy(pk_hbm.at[:, cols], keys.at[g], load_sem.at[2 * g]))
        loads.append(pltpu.make_async_copy(pv_hbm.at[:, cols], values.at[g], load_sem.at[2 * g + 1]))
    for load in loads:
        load.start()

    early.wait()
    own = q_in[...].astype(F32)
    for g in range(2):
        heads = [own[:, (4 * g + h) * HD : (4 * g + h + 1) * HD] for h in range(4)]
        q[g, p, z] = jnp.concatenate(heads, axis=0).astype(BF16)
    home = z // 2
    stays = home == t

    @pl.when(stays)
    def _():
        pl.semaphore_wait(barrier, NZ - 1 + NP - 1)

    @pl.when(jnp.logical_not(stays))
    def _():
        pl.semaphore_wait(barrier, NZ - 1 + NP - 1 + NZ)


    def q_z(g, k):
        block = q.at[g, p, z]
        return remote(block, block, qz_s.at[g], qz_r.at[g], at_z(k, 1) * NP + p, t)

    across = z * NP + (1 - y) * NX + x

    def wait_all(ref, sem):
        pltpu.make_async_copy(ref, ref, sem).wait()

    def q_x(g, j):
        block = q.at[g, plane(j - j % NX, -1)]
        return remote(block, block, qx_s.at[g], qx_r.at[g, j // NX], z * NP + plane(j % NX, 1), t)

    def q_half(g, side):
        j = 1 + 2 * side
        block = q.at[g, plane(j, -1), pl.ds(side * 4, 4)]
        return remote(block, block, qh_s.at[g], qh_r.at[g], z * NP + plane(j, 1), t)

    def q_y(g, j):
        block = q.at[g, plane(j, -1)]
        return remote(block, block, qy_s.at[g], qy_r.at[g, j // 2], across, t)

    def round_1(g):
        wait_all(q.at[g, 0, pl.ds(0, NZ - 1)], qz_r.at[g])
        q_x(g, 1).start()
        q_x(g, 3).start()
        q_y(g, 0).start()

    def round_2(g):
        wait_all(q.at[g, pl.ds(0, 2)], qx_r.at[g, 0])
        q_half(g, 0).start()
        q_half(g, 1).start()
        q_y(g, 0).wait_recv()
        q_x(g, 5).start()
        q_x(g, 7).start()

    def round_3(g):
        wait_all(q.at[g, 0], qh_r.at[g])
        q_y(g, 2).start()

    def pass_w(hop, sign):
        block = weights.at[at_z(hop - 1, -sign)]
        side = (1 - sign) // 2
        return remote(block, block, w_s.at[0], w_r.at[side, hop - 1], at_z(1, sign) * NP + p, t)

    for k in far_first:
        q_z(0, k).start()

    for load in loads:
        load.wait()
    leaf_length = lengths[z]
    pad = jnp.zeros((HD - 8, HD), F32)
    own_keys, own_values = sk_in[...].astype(F32), sv_in[...].astype(F32)
    for g in range(2):
        cols = slice(g * HD, (g + 1) * HD)
        sk[g] = jnp.concatenate([own_keys[:, cols], pad], axis=0).astype(BF16)
        sv[g] = jnp.concatenate([own_values[:, cols], pad], axis=0).astype(BF16)
    for leaf in range(NZ):
        current = jnp.int32(leaf)
        linked = jnp.int32(0)
        for _ in range(NZ):
            following = parents[current]
            hit = jnp.where(following != current, jnp.int32(1), jnp.int32(0))
            linked = jnp.maximum(linked, jnp.where(following == z, hit, jnp.int32(0)))
            current = following
        anc[leaf * LEAF_ROWS : (leaf + 1) * LEAF_ROWS, :] = jnp.full((LEAF_ROWS, HD), linked, jnp.int32)
    round_1(0)
    for k in far_first:
        q_z(1, k).start()
    pass_w(1, 1).start()
    pass_w(1, -1).start()

    row = lax.broadcasted_iota(jnp.int32, (ROWS, HD), 0)
    lane = lax.broadcasted_iota(jnp.int32, (ROWS, HD), 1)
    place = p * 8 + lane
    live = (lane < 8) & (place < leaf_length)
    same_leaf = (row // LEAF_ROWS) == z
    eye = lax.broadcasted_iota(jnp.int32, (HD, HD), 0) == lax.broadcasted_iota(jnp.int32, (HD, HD), 1)
    ones = jnp.ones((TILE, HD), BF16)

    def send_y(g, j):
        return remote(sums.at[g, NX + j], recv_y.at[g, j], ay_s.at[g], ay_r.at[g, j], across, t)

    def send_x(g, j):
        return remote(sums.at[g, j], recv_x.at[g, j], ax_s.at[g], ax_r.at[g], z * NP + plane(j, -1), t)

    def attend(g, group):
        blocks, masks = [], []
        for j in group:
            source = plane(j, -1)
            blocks.append(q[g, source].reshape(ROWS, HD))
            own_row = same_leaf & (place <= source * 8 + row % 8)
            masks.append(jnp.where(live & (own_row | (anc[...] > 0)), 1.0, 0.0))
        scaled = jnp.concatenate(blocks, axis=0).astype(F32) * SCALE
        hi = scaled.astype(BF16)
        low = (scaled - hi.astype(F32)).astype(BF16)
        query = jnp.concatenate([hi, low], axis=1)
        allowed = jnp.concatenate(masks, axis=0) > 0.5

        def scores(block):
            return lax.dot_general(
                query, jnp.concatenate([block, block], axis=1),
                (((1,), (1,)), ((), ())), preferred_element_type=F32,
            )

        leaf_scores = jnp.where(allowed, scores(sk[g]), LOW)
        following = scores(keys[g, 0:TILE, :])
        peak = jnp.max(leaf_scores, axis=1, keepdims=True)
        weight = jnp.where(allowed, jnp.exp2(leaf_scores - peak), 0.0).astype(BF16)
        total = jnp.dot(
            weight, jnp.concatenate([sv[g], ones[:HD]], axis=1), preferred_element_type=F32
        )
        for tile in range(KEYS // TILE):
            now = following
            raised = jnp.maximum(peak, jnp.max(now, axis=1, keepdims=True))
            if tile + 1 < KEYS // TILE:
                following = scores(keys[g, (tile + 1) * TILE : (tile + 2) * TILE, :])
            weight = jnp.exp2(now - raised).astype(BF16)
            table = jnp.concatenate([values[g, tile * TILE : (tile + 1) * TILE, :], ones], axis=1)
            total = total * jnp.exp2(peak - raised) + jnp.dot(weight, table, preferred_element_type=F32)
            peak = raised
        mean = (total[:, :HD] / total[:, HD:]).astype(BF16)
        lam = (peak + jnp.log2(total[:, HD:])).reshape(len(group), 2, HD, HD)
        lam = jnp.sum(jnp.where(eye[None, None], lam, 0.0), axis=2)
        for i, j in enumerate(group):
            sums[g, j, 0:ROWS, :] = mean[i * ROWS : (i + 1) * ROWS]
            sums[g, j, ROWS : ROWS + TAIL, :] = pack_tail(lam[i])

    def send_b(g, k):
        return remote(
            part_b.at[g, at_z(k, 1)], recv_b.at[g, k], b_s.at[g], b_r.at[g], at_z(k, 1) * NP + p, t
        )

    def merge_pair(g, j):
        send_y(g, j).wait_recv()
        ours, theirs = sums.at[g, j], recv_y.at[g, j]
        lam_a, lam_b = read_tail(ours[ROWS : ROWS + TAIL, :]), read_tail(theirs[ROWS : ROWS + TAIL, :])
        peak = jnp.maximum(lam_a, lam_b)
        whole = peak + jnp.log2(jnp.exp2(lam_a - peak) + jnp.exp2(lam_b - peak))
        weight = jnp.exp2(lam_a - whole)
        for half in range(2):
            span = slice(half * HD, (half + 1) * HD)
            column = jnp.sum(jnp.where(eye, weight[half : half + 1], 0.0), axis=1, keepdims=True)
            a, b = ours[span, :].astype(F32), theirs[span, :].astype(F32)
            ours[span, :] = (b + column * (a - b)).astype(BF16)
        ours[ROWS : ROWS + TAIL, :] = pack_tail(whole)
        if j:
            send_x(g, j).start()

    def merge_plane(g):
        wait_all(recv_x.at[g, pl.ds(1, NX - 1)], ax_r.at[g])
        held = [sums.at[g, 0]] + [recv_x.at[g, j] for j in range(1, NX)]
        lams = [read_tail(block[ROWS : ROWS + TAIL, :]) for block in held]
        peak = lams[0]
        for lam in lams[1:]:
            peak = jnp.maximum(peak, lam)
        weights = [jnp.exp2(lam - peak) for lam in lams]
        whole = sum(weights[1:], weights[0])
        tail = pack_tail(peak + jnp.log2(whole))
        weights = [weight / whole for weight in weights]
        for half in range(2):
            merged = None
            for block, weight in zip(held, weights):
                column = jnp.sum(jnp.where(eye, weight[half : half + 1], 0.0), axis=1, keepdims=True)
                term = column * block[half * HD : (half + 1) * HD, :].astype(F32)
                merged = term if merged is None else merged + term
            merged = merged.astype(BF16)
            for i in range(4):
                part_b[g, 4 * half + i, 0:LEAF_ROWS, :] = merged[i * LEAF_ROWS : (i + 1) * LEAF_ROWS]
                part_b[g, 4 * half + i, LEAF_ROWS : LEAF_ROWS + TAIL, :] = tail
        for k in far_first:
            send_b(g, k).start()

    def att_p(g, j):
        block = att.at[g, p]
        return remote(block, block, c_s.at[g], c_r.at[g], z * NP + plane(j, 1), t)

    def merge_z(g):
        wait_all(recv_b.at[g, pl.ds(1, NZ - 1)], b_r.at[g])
        shape = (LEAF_ROWS, HD)
        spot = lax.broadcasted_iota(jnp.int32, shape, 1) == (
            lax.broadcasted_iota(jnp.int32, shape, 0) + LEAF_ROWS * (z % 4)
        )
        held = [part_b[g, z]] + [recv_b[g, k] for k in range(1, NZ)]
        lams = []
        for block in held:
            lam = read_tail(block[LEAF_ROWS : LEAF_ROWS + TAIL])
            line = jnp.where(z // 4 == 0, lam[0:1], lam[1:2])
            lams.append(jnp.sum(jnp.where(spot, line, 0.0), axis=1, keepdims=True))
        peak = lams[0]
        for lam in lams[1:]:
            peak = jnp.maximum(peak, lam)
        top, whole = None, None
        for block, lam in zip(held, lams):
            weight = jnp.exp2(lam - peak)
            term = weight * block[:LEAF_ROWS].astype(F32)
            top = term if top is None else top + term
            whole = weight if whole is None else whole + weight
        att[g, p] = (top / whole).astype(BF16)
        for j in (6, 5, 7, 2, 4, 1, 3):
            att_p(g, j).start()

    def project(g):
        wait_all(att.at[g, pl.ds(0, NP - 1)], c_r.at[g])
        rows = [att[g, source].astype(F32) for source in range(NP)]
        heads = []
        for h in range(4):
            heads.append(jnp.concatenate([block[8 * h : 8 * h + 8] for block in rows], axis=0))
        tokens = jnp.concatenate(heads, axis=1).astype(BF16)
        table = weights[:, :, g * 4 * HD : (g + 1) * 4 * HD].reshape(NZ * 64, 4 * HD)
        return lax.dot_general(table, tokens, (((1,), (1,)), ((), ())), preferred_element_type=F32)

    def step(i, carry):
        def of_step(table):
            return sum(entry * (1 // (1 + (i - s) * (i - s))) for s, entry in enumerate(table) if entry)

        g = i // 5
        first = of_step((0, 1, 4, 5, 2, 5, 6, 3, 4, 0))
        second = of_step((0, 3, 0, 7, 6, 7, 1, 2, 0, 0))
        single = (i == 0) | (i == 2) | (i >= 8)

        @pl.when(i == 1)
        def _():
            round_2(0)
            round_1(1)

        @pl.when(i == 2)
        def _():
            round_3(0)

        @pl.when(i == 3)
        def _():
            round_2(1)
            wait_all(q.at[0, pl.ds(0, 2)], qx_r.at[0, 1])

        @pl.when(i == 4)
        def _():
            q_y(0, 2).wait_recv()
            round_3(1)

        @pl.when(i == 5)
        def _():
            wait_all(q.at[1, pl.ds(0, 2)], qx_r.at[1, 1])

        @pl.when(i == 6)
        def _():
            q_y(1, 2).wait_recv()

        for hop in (2, 3, 4):

            @pl.when(i == 2 * hop - 1)
            def _():
                pass_w(hop - 1, 1).wait_recv()
                pass_w(hop, 1).start()
                pass_w(hop - 1, -1).wait_recv()
                if hop < 4:
                    pass_w(hop, -1).start()

        @pl.when(i == 7)
        def _():
            for j in (2, 1, 3, 0):
                merge_pair(0, j)

        @pl.when(i == 8)
        def _():
            merge_pair(1, 1)
            merge_pair(1, 3)
            merge_pair(1, 2)

        @pl.when(single)
        def _():
            attend(g, (first,))

        @pl.when(jnp.logical_not(single))
        def _():
            attend(g, (first, second))

            @pl.when(second >= NX)
            def _():
                send_y(g, second - NX).start()

        @pl.when(first >= NX)
        def _():
            send_y(g, first - NX).start()

        return carry

    lax.fori_loop(0, 10, step, 0)
    merge_plane(0)
    merge_pair(1, 0)
    merge_plane(1)
    merge_z(0)
    merge_z(1)
    pass_w(4, 1).wait_recv()
    projected = project(0)
    projected = projected + project(1)
    for k in range(NZ):
        block = projected[64 * k : 64 * k + 64]
        shares_out[k] = jnp.concatenate([block[:32], block[32:]], axis=1).astype(BF16)

    slot = (z % 2) * NT + t

    def share(k):
        to = at_z(k, 1)
        return remote(shares_out.at[to], shares_in.at[slot], d_s.at[1 // (k + 1)], d_r.at[slot], to * NP + p, home)

    for k in far_first:
        share(k).start()

    @pl.when(jnp.logical_not(stays))
    def _():
        share(0).start()

    @pl.when(stays)
    def _():
        shares_in[slot] = shares_out[z]

    for side in range(2):
        for i in range(NT):

            @pl.when(jnp.logical_not((2 * t + side == z) & (t == i)))
            def _():
                here = shares_in.at[side * NT + i]
                remote(here, here, d_s.at[0], d_r.at[side * NT + i], (2 * t + side) * NP + p, i).wait_recv()

    sides = []
    for side in range(2):
        parts = [shares_in[side * NT + i].astype(F32) for i in range(NT)]
        sides.append((parts[0] + parts[1]) + (parts[2] + parts[3]))
    top = jnp.concatenate([sides[0][:, :64], sides[1][:, :64]], axis=1)
    bottom = jnp.concatenate([sides[0][:, 64:], sides[1][:, 64:]], axis=1)
    out_ref[0:32, :] = (res_in[0:32, :].astype(F32) + top).astype(BF16)
    out_ref[32:64, :] = (res_in[32:64, :].astype(F32) + bottom).astype(BF16)

    for g in range(2):
        wait_all(q.at[g, 0, pl.ds(0, NZ - 1)], qz_s.at[g])
        wait_all(q.at[g, pl.ds(0, 4)], qx_s.at[g])
        wait_all(q.at[g, 0], qh_s.at[g])
        wait_all(q.at[g, pl.ds(0, 2)], qy_s.at[g])
        wait_all(sums.at[g, pl.ds(0, NX)], ay_s.at[g])
        wait_all(sums.at[g, pl.ds(0, NX - 1)], ax_s.at[g])
        wait_all(part_b.at[g, pl.ds(0, NZ - 1)], b_s.at[g])
        wait_all(att.at[g, pl.ds(0, NP - 1)], c_s.at[g])
    wait_all(weights.at[pl.ds(0, NZ - 1)], w_s.at[0])
    wait_all(shares_out.at[pl.ds(0, NZ - 1)], d_s.at[0])

    @pl.when(jnp.logical_not(stays))
    def _():
        share(0).wait_send()


def shards(queries, suffix_keys, suffix_values, prefix_keys, prefix_values, lengths, parents, out_weight, residual):
    hbm = pl.BlockSpec(memory_space=pltpu.HBM)
    dma = pltpu.SemaphoreType.DMA
    flipped = pl.pallas_call(
        kernel,
        out_shape=jax.ShapeDtypeStruct(residual.shape[::-1], BF16),
        in_specs=[hbm] * 9,
        out_specs=pl.BlockSpec(memory_space=pltpu.VMEM),
        scratch_shapes=[
            pltpu.SMEM((8,), jnp.int32),
            pltpu.SMEM((8,), jnp.int32),
            pltpu.VMEM((8, 8 * HD), BF16),
            pltpu.VMEM((8, 2 * HD), BF16),
            pltpu.VMEM((8, 2 * HD), BF16),
            pltpu.VMEM((64, HD), BF16),
            pltpu.VMEM((2, KEYS, HD), BF16),
            pltpu.VMEM((2, KEYS, HD), BF16),
            pltpu.VMEM((NZ, 64, 8 * HD), BF16),
            pltpu.VMEM((2, HD, HD), BF16),
            pltpu.VMEM((2, HD, HD), BF16),
            pltpu.VMEM((ROWS, HD), jnp.int32),
            pltpu.VMEM((2, NP, NZ, LEAF_ROWS, HD), BF16),
            pltpu.VMEM((2, NP, ROWS + TAIL, HD), BF16),
            pltpu.VMEM((2, NX, ROWS + TAIL, HD), BF16),
            pltpu.VMEM((2, NX, ROWS + TAIL, HD), BF16),
            pltpu.VMEM((2, NZ, LEAF_ROWS + TAIL, HD), BF16),
            pltpu.VMEM((2, NZ, LEAF_ROWS + TAIL, HD), BF16),
            pltpu.VMEM((2, NP, LEAF_ROWS, HD), BF16),
            pltpu.VMEM((NZ, 32, HD), BF16),
            pltpu.VMEM((2 * NT, 32, HD), BF16),
            dma((11,)),
            dma((2,)), dma((2,)),
            dma((2,)), dma((2, 2)),
            dma((2,)), dma((2,)),
            dma((2,)), dma((2, 2)),
            dma((1,)), dma((2, 4)),
            dma((2,)), dma((2, NX)),
            dma((2,)), dma((2,)),
            dma((2,)), dma((2,)),
            dma((2,)), dma((2,)),
            dma((2,)), dma((2 * NT,)),
        ],
        compiler_params=pltpu.CompilerParams(
            collective_id=0, has_side_effects=True, vmem_limit_bytes=(64 << 20) - (64 << 10)
        ),
        cost_estimate=pl.CostEstimate(
            flops=18 << 30, bytes_accessed=5 << 20, transcendentals=17 << 20
        ),
        name="cascade",
    )(lengths, parents, queries, suffix_keys, suffix_values, prefix_keys, prefix_values, out_weight.T, residual.T)
    return flipped.T


def solution(mesh):
    placed = (
        P("ctx", "tp"), P("ctx", "tp"), P("ctx", "tp"), P("ctx", "tp"), P("ctx", "tp"),
        P(), P(), P("tp", "ctx"), P("tp", "ctx"),
    )
    return jax.shard_map(shards, mesh=mesh, in_specs=placed, out_specs=P("tp", "ctx"), check_vma=False)
```

```python
import math

import jax
import jax.numpy as jnp
from jax import lax
from jax.experimental import pallas as pl
from jax.experimental.pallas import tpu as pltpu
from jax.sharding import PartitionSpec as P

HD = 128
NX, NY, NZ = 4, 2, 8
NP = NX * NY
NT = 4
LEAF_ROWS = 32
ROWS = NZ * LEAF_ROWS
TAIL = 16
KEYS = 4096
TILE = 1024
SCALE = math.log2(math.e) / math.sqrt(HD)
LOW = -1e30
F32, BF16 = jnp.float32, jnp.bfloat16
MESH = pl.DeviceIdType.MESH


def split3(x):
    hi = x.astype(BF16).astype(F32)
    rest = x - hi
    mid = rest.astype(BF16).astype(F32)
    low = (rest - mid).astype(BF16).astype(F32)
    return hi, mid, low


def pack_tail(lam):
    zeros = jnp.zeros((TAIL - 6, 128), F32)
    return jnp.concatenate([*split3(lam), zeros], axis=0).astype(BF16)


def read_tail(tail):
    tail = tail.astype(F32)
    return tail[0:2] + tail[2:4] + tail[4:6]


def kernel(
    lengths_in, parents_in, q_hbm, sk_hbm, sv_hbm, pk_hbm, pv_hbm, w_hbm, res_hbm, out_ref,
    lengths, parents, q_in, sk_in, sv_in, res_in, keys, values, weights, sk, sv, anc, q, sums, recv_y, recv_x, part_b, recv_b, att,
    shares_out, shares_in,
    load_sem, qz_s, qz_r, qx_s, qx_r, qh_s, qh_r, qy_s, qy_r, w_s, w_r, ay_s, ay_r, ax_s, ax_r, b_s, b_r, c_s, c_r, d_s, d_r,
):
    far_first = (4, 3, 5, 2, 6, 1, 7)
    c, t = lax.axis_index("ctx"), lax.axis_index("tp")
    z, p = c // NP, c % NP
    y, x = p // NX, p % NX

    def plane(j, sign):
        xx = (x + NX + sign * (j % NX)) % NX
        yy = (y + NY + sign * (j // NX)) % NY
        return yy * NX + xx

    def at_z(k, sign):
        return (z + NZ + sign * k) % NZ

    def remote(src, dst, send, recv, ctx, tp):
        return pltpu.make_async_remote_copy(
            src_ref=src, dst_ref=dst, send_sem=send, recv_sem=recv,
            device_id=(ctx, tp), device_id_type=MESH,
        )

    early = pltpu.make_async_copy(q_hbm, q_in, load_sem.at[4])
    early.start()
    barrier = pltpu.get_barrier_semaphore()
    for k in far_first:
        pl.semaphore_signal(barrier, inc=1, device_id=(at_z(k, 1) * NP + p, t), device_id_type=MESH)
    for j in range(1, NP):
        pl.semaphore_signal(barrier, inc=1, device_id=(z * NP + plane(j, 1), t), device_id_type=MESH)
    for side in range(2):
        for i in range(1, NT):
            there = ((2 * t + side) * NP + p, (t + i) % NT)
            pl.semaphore_signal(barrier, inc=1, device_id=there, device_id_type=MESH)

    loads = []
    for k, (src, dst) in enumerate(
        ((lengths_in, lengths), (parents_in, parents), (sk_hbm, sk_in), (sv_hbm, sv_in), (w_hbm, weights.at[z]), (res_hbm, res_in))
    ):
        loads.append(pltpu.make_async_copy(src, dst, load_sem.at[5 + k]))
    for g in range(2):
        cols = pl.ds(g * HD, HD)
        loads.append(pltpu.make_async_copy(pk_hbm.at[:, cols], keys.at[g], load_sem.at[2 * g]))
        loads.append(pltpu.make_async_copy(pv_hbm.at[:, cols], values.at[g], load_sem.at[2 * g + 1]))
    for load in loads:
        load.start()

    early.wait()
    own = q_in[...].astype(F32)
    for g in range(2):
        heads = [own[:, (4 * g + h) * HD : (4 * g + h + 1) * HD] for h in range(4)]
        q[g, p, z] = jnp.concatenate(heads, axis=0).astype(BF16)
    home = z // 2
    stays = home == t

    @pl.when(stays)
    def _():
        pl.semaphore_wait(barrier, NZ - 1 + NP - 1)

    @pl.when(jnp.logical_not(stays))
    def _():
        pl.semaphore_wait(barrier, NZ - 1 + NP - 1 + NZ)


    def q_z(g, k):
        block = q.at[g, p, z]
        return remote(block, block, qz_s.at[g], qz_r.at[g], at_z(k, 1) * NP + p, t)

    across = z * NP + (1 - y) * NX + x

    def wait_all(ref, sem):
        pltpu.make_async_copy(ref, ref, sem).wait()

    def q_x(g, j):
        block = q.at[g, plane(j - j % NX, -1)]
        return remote(block, block, qx_s.at[g], qx_r.at[g, j // NX], z * NP + plane(j % NX, 1), t)

    def q_half(g, side):
        j = 1 + 2 * side
        block = q.at[g, plane(j, -1), pl.ds(side * 4, 4)]
        return remote(block, block, qh_s.at[g], qh_r.at[g], z * NP + plane(j, 1), t)

    def q_y(g, j):
        block = q.at[g, plane(j, -1)]
        return remote(block, block, qy_s.at[g], qy_r.at[g, j // 2], across, t)

    def round_1(g):
        wait_all(q.at[g, 0, pl.ds(0, NZ - 1)], qz_r.at[g])
        q_x(g, 1).start()
        q_x(g, 3).start()
        q_y(g, 0).start()

    def round_2(g):
        wait_all(q.at[g, pl.ds(0, 2)], qx_r.at[g, 0])
        q_half(g, 0).start()
        q_half(g, 1).start()
        q_y(g, 0).wait_recv()
        q_x(g, 5).start()
        q_x(g, 7).start()

    def round_3(g):
        wait_all(q.at[g, 0], qh_r.at[g])
        q_y(g, 2).start()

    def pass_w(hop, sign):
        block = weights.at[at_z(hop - 1, -sign)]
        side = (1 - sign) // 2
        return remote(block, block, w_s.at[0], w_r.at[side, hop - 1], at_z(1, sign) * NP + p, t)

    for k in far_first:
        q_z(0, k).start()

    for load in loads:
        load.wait()
    leaf_length = lengths[z]
    pad = jnp.zeros((HD - 8, HD), F32)
    own_keys, own_values = sk_in[...].astype(F32), sv_in[...].astype(F32)
    for g in range(2):
        cols = slice(g * HD, (g + 1) * HD)
        sk[g] = jnp.concatenate([own_keys[:, cols], pad], axis=0).astype(BF16)
        sv[g] = jnp.concatenate([own_values[:, cols], pad], axis=0).astype(BF16)
    for leaf in range(NZ):
        current = jnp.int32(leaf)
        linked = jnp.int32(0)
        for _ in range(NZ):
            following = parents[current]
            hit = jnp.where(following != current, jnp.int32(1), jnp.int32(0))
            linked = jnp.maximum(linked, jnp.where(following == z, hit, jnp.int32(0)))
            current = following
        anc[leaf * LEAF_ROWS : (leaf + 1) * LEAF_ROWS, :] = jnp.full((LEAF_ROWS, HD), linked, jnp.int32)
    round_1(0)
    for k in far_first:
        q_z(1, k).start()
    pass_w(1, 1).start()
    pass_w(1, -1).start()

    row = lax.broadcasted_iota(jnp.int32, (ROWS, HD), 0)
    lane = lax.broadcasted_iota(jnp.int32, (ROWS, HD), 1)
    place = p * 8 + lane
    live = (lane < 8) & (place < leaf_length)
    same_leaf = (row // LEAF_ROWS) == z
    eye = lax.broadcasted_iota(jnp.int32, (HD, HD), 0) == lax.broadcasted_iota(jnp.int32, (HD, HD), 1)
    ones = jnp.ones((TILE, HD), BF16)

    def send_y(g, j):
        return remote(sums.at[g, NX + j], recv_y.at[g, j], ay_s.at[g], ay_r.at[g, j], across, t)

    def send_x(g, j):
        return remote(sums.at[g, j], recv_x.at[g, j], ax_s.at[g], ax_r.at[g], z * NP + plane(j, -1), t)

    def attend(g, group):
        blocks, masks = [], []
        for j in group:
            source = plane(j, -1)
            blocks.append(q[g, source].reshape(ROWS, HD))
            own_row = same_leaf & (place <= source * 8 + row % 8)
            masks.append(jnp.where(live & (own_row | (anc[...] > 0)), 1.0, 0.0))
        scaled = jnp.concatenate(blocks, axis=0).astype(F32) * SCALE
        hi = scaled.astype(BF16)
        low = (scaled - hi.astype(F32)).astype(BF16)
        query = jnp.concatenate([hi, low], axis=1)
        allowed = jnp.concatenate(masks, axis=0) > 0.5

        def scores(block):
            return lax.dot_general(
                query, jnp.concatenate([block, block], axis=1),
                (((1,), (1,)), ((), ())), preferred_element_type=F32,
            )

        leaf_scores = jnp.where(allowed, scores(sk[g]), LOW)
        following = scores(keys[g, 0:TILE, :])
        peak = jnp.max(leaf_scores, axis=1, keepdims=True)
        weight = jnp.where(allowed, jnp.exp2(leaf_scores - peak), 0.0).astype(BF16)
        total = jnp.dot(
            weight, jnp.concatenate([sv[g], ones[:HD]], axis=1), preferred_element_type=F32
        )
        for tile in range(KEYS // TILE):
            now = following
            raised = jnp.maximum(peak, jnp.max(now, axis=1, keepdims=True))
            if tile + 1 < KEYS // TILE:
                following = scores(keys[g, (tile + 1) * TILE : (tile + 2) * TILE, :])
            weight = jnp.exp2(now - raised).astype(BF16)
            table = jnp.concatenate([values[g, tile * TILE : (tile + 1) * TILE, :], ones], axis=1)
            total = total * jnp.exp2(peak - raised) + jnp.dot(weight, table, preferred_element_type=F32)
            peak = raised
        mean = (total[:, :HD] / total[:, HD:]).astype(BF16)
        lam = (peak + jnp.log2(total[:, HD:])).reshape(len(group), 2, HD, HD)
        lam = jnp.sum(jnp.where(eye[None, None], lam, 0.0), axis=2)
        for i, j in enumerate(group):
            sums[g, j, 0:ROWS, :] = mean[i * ROWS : (i + 1) * ROWS]
            sums[g, j, ROWS : ROWS + TAIL, :] = pack_tail(lam[i])

    def send_b(g, k):
        return remote(
            part_b.at[g, at_z(k, 1)], recv_b.at[g, k], b_s.at[g], b_r.at[g], at_z(k, 1) * NP + p, t
        )

    def merge_pair(g, j):
        send_y(g, j).wait_recv()
        ours, theirs = sums.at[g, j], recv_y.at[g, j]
        lam_a, lam_b = read_tail(ours[ROWS : ROWS + TAIL, :]), read_tail(theirs[ROWS : ROWS + TAIL, :])
        peak = jnp.maximum(lam_a, lam_b)
        whole = peak + jnp.log2(jnp.exp2(lam_a - peak) + jnp.exp2(lam_b - peak))
        weight = jnp.exp2(lam_a - whole)
        for half in range(2):
            span = slice(half * HD, (half + 1) * HD)
            column = jnp.sum(jnp.where(eye, weight[half : half + 1], 0.0), axis=1, keepdims=True)
            a, b = ours[span, :].astype(F32), theirs[span, :].astype(F32)
            ours[span, :] = (b + column * (a - b)).astype(BF16)
        ours[ROWS : ROWS + TAIL, :] = pack_tail(whole)
        if j:
            send_x(g, j).start()

    def merge_plane(g):
        wait_all(recv_x.at[g, pl.ds(1, NX - 1)], ax_r.at[g])
        held = [sums.at[g, 0]] + [recv_x.at[g, j] for j in range(1, NX)]
        lams = [read_tail(block[ROWS : ROWS + TAIL, :]) for block in held]
        peak = lams[0]
        for lam in lams[1:]:
            peak = jnp.maximum(peak, lam)
        weights = [jnp.exp2(lam - peak) for lam in lams]
        whole = sum(weights[1:], weights[0])
        tail = pack_tail(peak + jnp.log2(whole))
        weights = [weight / whole for weight in weights]
        for half in range(2):
            merged = None
            for block, weight in zip(held, weights):
                column = jnp.sum(jnp.where(eye, weight[half : half + 1], 0.0), axis=1, keepdims=True)
                term = column * block[half * HD : (half + 1) * HD, :].astype(F32)
                merged = term if merged is None else merged + term
            merged = merged.astype(BF16)
            for i in range(4):
                part_b[g, 4 * half + i, 0:LEAF_ROWS, :] = merged[i * LEAF_ROWS : (i + 1) * LEAF_ROWS]
                part_b[g, 4 * half + i, LEAF_ROWS : LEAF_ROWS + TAIL, :] = tail
        for k in far_first:
            send_b(g, k).start()

    def att_p(g, j):
        block = att.at[g, p]
        return remote(block, block, c_s.at[g], c_r.at[g], z * NP + plane(j, 1), t)

    def merge_z(g):
        wait_all(recv_b.at[g, pl.ds(1, NZ - 1)], b_r.at[g])
        shape = (LEAF_ROWS, HD)
        spot = lax.broadcasted_iota(jnp.int32, shape, 1) == (
            lax.broadcasted_iota(jnp.int32, shape, 0) + LEAF_ROWS * (z % 4)
        )
        held = [part_b[g, z]] + [recv_b[g, k] for k in range(1, NZ)]
        lams = []
        for block in held:
            lam = read_tail(block[LEAF_ROWS : LEAF_ROWS + TAIL])
            line = jnp.where(z // 4 == 0, lam[0:1], lam[1:2])
            lams.append(jnp.sum(jnp.where(spot, line, 0.0), axis=1, keepdims=True))
        peak = lams[0]
        for lam in lams[1:]:
            peak = jnp.maximum(peak, lam)
        top, whole = None, None
        for block, lam in zip(held, lams):
            weight = jnp.exp2(lam - peak)
            term = weight * block[:LEAF_ROWS].astype(F32)
            top = term if top is None else top + term
            whole = weight if whole is None else whole + weight
        att[g, p] = (top / whole).astype(BF16)
        for j in (6, 5, 7, 2, 4, 1, 3):
            att_p(g, j).start()

    def project(g):
        wait_all(att.at[g, pl.ds(0, NP - 1)], c_r.at[g])
        rows = [att[g, source].astype(F32) for source in range(NP)]
        heads = []
        for h in range(4):
            heads.append(jnp.concatenate([block[8 * h : 8 * h + 8] for block in rows], axis=0))
        tokens = jnp.concatenate(heads, axis=1).astype(BF16)
        table = weights[:, :, g * 4 * HD : (g + 1) * 4 * HD].reshape(NZ * 64, 4 * HD)
        return lax.dot_general(table, tokens, (((1,), (1,)), ((), ())), preferred_element_type=F32)

    def step(i, carry):
        def of_step(table):
            return sum(entry * (1 // (1 + (i - s) * (i - s))) for s, entry in enumerate(table) if entry)

        g = i // 5
        first = of_step((0, 1, 4, 5, 2, 5, 6, 3, 4, 0))
        second = of_step((0, 3, 0, 7, 6, 7, 1, 2, 0, 0))
        single = (i == 0) | (i == 2) | (i >= 8)

        @pl.when(i == 1)
        def _():
            round_2(0)
            round_1(1)

        @pl.when(i == 2)
        def _():
            round_3(0)

        @pl.when(i == 3)
        def _():
            round_2(1)
            wait_all(q.at[0, pl.ds(0, 2)], qx_r.at[0, 1])

        @pl.when(i == 4)
        def _():
            q_y(0, 2).wait_recv()
            round_3(1)

        @pl.when(i == 5)
        def _():
            wait_all(q.at[1, pl.ds(0, 2)], qx_r.at[1, 1])

        @pl.when(i == 6)
        def _():
            q_y(1, 2).wait_recv()

        for hop in (2, 3, 4):

            @pl.when(i == 2 * hop - 1)
            def _():
                pass_w(hop - 1, 1).wait_recv()
                pass_w(hop, 1).start()
                pass_w(hop - 1, -1).wait_recv()
                if hop < 4:
                    pass_w(hop, -1).start()

        @pl.when(i == 7)
        def _():
            for j in (2, 1, 3, 0):
                merge_pair(0, j)

        @pl.when(i == 8)
        def _():
            merge_pair(1, 1)
            merge_pair(1, 3)
            merge_pair(1, 2)

        @pl.when(single)
        def _():
            attend(g, (first,))

        @pl.when(jnp.logical_not(single))
        def _():
            attend(g, (first, second))

            @pl.when(second >= NX)
            def _():
                send_y(g, second - NX).start()

        @pl.when(first >= NX)
        def _():
            send_y(g, first - NX).start()

        return carry

    lax.fori_loop(0, 10, step, 0)
    merge_plane(0)
    merge_pair(1, 0)
    merge_plane(1)
    merge_z(0)
    merge_z(1)
    pass_w(4, 1).wait_recv()
    projected = project(0)
    projected = projected + project(1)
    for k in range(NZ):
        block = projected[64 * k : 64 * k + 64]
        shares_out[k] = jnp.concatenate([block[:32], block[32:]], axis=1).astype(BF16)

    slot = (z % 2) * NT + t

    def share(k):
        to = at_z(k, 1)
        return remote(shares_out.at[to], shares_in.at[slot], d_s.at[1 // (k + 1)], d_r.at[slot], to * NP + p, home)

    for k in far_first:
        share(k).start()

    @pl.when(jnp.logical_not(stays))
    def _():
        share(0).start()

    @pl.when(stays)
    def _():
        shares_in[slot] = shares_out[z]

    for side in range(2):
        for i in range(NT):

            @pl.when(jnp.logical_not((2 * t + side == z) & (t == i)))
            def _():
                here = shares_in.at[side * NT + i]
                remote(here, here, d_s.at[0], d_r.at[side * NT + i], (2 * t + side) * NP + p, i).wait_recv()

    sides = []
    for side in range(2):
        parts = [shares_in[side * NT + i].astype(F32) for i in range(NT)]
        sides.append((parts[0] + parts[1]) + (parts[2] + parts[3]))
    top = jnp.concatenate([sides[0][:, :64], sides[1][:, :64]], axis=1)
    bottom = jnp.concatenate([sides[0][:, 64:], sides[1][:, 64:]], axis=1)
    state = res_in[...].astype(F32) + jnp.concatenate([top, bottom], axis=0)
    out_ref[...] = state.T.astype(BF16)

    for g in range(2):
        wait_all(q.at[g, 0, pl.ds(0, NZ - 1)], qz_s.at[g])
        wait_all(q.at[g, pl.ds(0, 4)], qx_s.at[g])
        wait_all(q.at[g, 0], qh_s.at[g])
        wait_all(q.at[g, pl.ds(0, 2)], qy_s.at[g])
        wait_all(sums.at[g, pl.ds(0, NX)], ay_s.at[g])
        wait_all(sums.at[g, pl.ds(0, NX - 1)], ax_s.at[g])
        wait_all(part_b.at[g, pl.ds(0, NZ - 1)], b_s.at[g])
        wait_all(att.at[g, pl.ds(0, NP - 1)], c_s.at[g])
    wait_all(weights.at[pl.ds(0, NZ - 1)], w_s.at[0])
    wait_all(shares_out.at[pl.ds(0, NZ - 1)], d_s.at[0])

    @pl.when(jnp.logical_not(stays))
    def _():
        share(0).wait_send()


def shards(queries, suffix_keys, suffix_values, prefix_keys, prefix_values, lengths, parents, out_weight, residual):
    hbm = pl.BlockSpec(memory_space=pltpu.HBM)
    dma = pltpu.SemaphoreType.DMA
    return pl.pallas_call(
        kernel,
        out_shape=jax.ShapeDtypeStruct(residual.shape, BF16),
        in_specs=[hbm] * 9,
        out_specs=pl.BlockSpec(memory_space=pltpu.VMEM),
        scratch_shapes=[
            pltpu.SMEM((8,), jnp.int32),
            pltpu.SMEM((8,), jnp.int32),
            pltpu.VMEM((8, 8 * HD), BF16),
            pltpu.VMEM((8, 2 * HD), BF16),
            pltpu.VMEM((8, 2 * HD), BF16),
            pltpu.VMEM((64, HD), BF16),
            pltpu.VMEM((2, KEYS, HD), BF16),
            pltpu.VMEM((2, KEYS, HD), BF16),
            pltpu.VMEM((NZ, 64, 8 * HD), BF16),
            pltpu.VMEM((2, HD, HD), BF16),
            pltpu.VMEM((2, HD, HD), BF16),
            pltpu.VMEM((ROWS, HD), jnp.int32),
            pltpu.VMEM((2, NP, NZ, LEAF_ROWS, HD), BF16),
            pltpu.VMEM((2, NP, ROWS + TAIL, HD), BF16),
            pltpu.VMEM((2, NX, ROWS + TAIL, HD), BF16),
            pltpu.VMEM((2, NX, ROWS + TAIL, HD), BF16),
            pltpu.VMEM((2, NZ, LEAF_ROWS + TAIL, HD), BF16),
            pltpu.VMEM((2, NZ, LEAF_ROWS + TAIL, HD), BF16),
            pltpu.VMEM((2, NP, LEAF_ROWS, HD), BF16),
            pltpu.VMEM((NZ, 32, HD), BF16),
            pltpu.VMEM((2 * NT, 32, HD), BF16),
            dma((11,)),
            dma((2,)), dma((2,)),
            dma((2,)), dma((2, 2)),
            dma((2,)), dma((2,)),
            dma((2,)), dma((2, 2)),
            dma((1,)), dma((2, 4)),
            dma((2,)), dma((2, NX)),
            dma((2,)), dma((2,)),
            dma((2,)), dma((2,)),
            dma((2,)), dma((2,)),
            dma((2,)), dma((2 * NT,)),
        ],
        compiler_params=pltpu.CompilerParams(
            collective_id=0, has_side_effects=True, vmem_limit_bytes=(64 << 20) - (64 << 10)
        ),
        cost_estimate=pl.CostEstimate(
            flops=18 << 30, bytes_accessed=5 << 20, transcendentals=17 << 20
        ),
        name="cascade",
    )(lengths, parents, queries, suffix_keys, suffix_values, prefix_keys, prefix_values, out_weight.T, residual.T)


def solution(mesh):
    placed = (
        P("ctx", "tp"), P("ctx", "tp"), P("ctx", "tp"), P("ctx", "tp"), P("ctx", "tp"),
        P(), P(), P("tp", "ctx"), P("tp", "ctx"),
    )
    return jax.shard_map(shards, mesh=mesh, in_specs=placed, out_specs=P("tp", "ctx"), check_vma=False)
```
